32 devices in a mesh: shots: 2 (over x), gx: 8 (over z, y), gy: 2 (over core).
Axes of the slice: x: 2, y: 2, z: 4, core: 2. Of those that a mesh axis runs over, the one named last changes fastest.
Arguments:
- field_now: float32 [512, 96, 128], P(('shots', 'gx'), 'gy'), parts along dimension 0, may hold values from -6 to 6
- field_prev: float32 [512, 96, 128], P(('shots', 'gx'), 'gy'), parts along dimension 0, may hold values from -6 to 6
- courant_squared: float32 [256, 96, 128], P('gx', 'gy'), may hold values from 0.05 to 0.18, as said below
- source_cells: int32 [3, 16], P(None, 'shots'), parts along dimension 1, may hold values from 0 to 127, as said below
- source_wave: float32 [4, 16], P(None, 'shots'), parts along dimension 1, may hold values from -8 to 8
- receiver_cells: int32 [3, 512], P(None, 'shots'), parts along dimension 1, may hold values from 0 to 127, as said below
- receiver_wave: float32 [4, 512], P(None, 'shots'), parts along dimension 1, may hold values from -8 to 8
- snapshot_steps: int32 [4, 2], P('shots'), parts along dimension 0, may hold values from 1 to 4, as said below
- lag_offsets: int32 [17], replicated, may hold values from -8 to 8
Outputs:
- final_field: float32 [512, 96, 128], P(('shots', 'gx'), 'gy'), parts along dimension 0
- extended_image: float32 [256, 17, 1536], P(('shots', 'gx'), None, 'gy'), parts along dimension 0
The draws below stay inside these ranges and needn't reach their ends.
There are 2 independent parts, one for each index of `shots`. The reference program is written for one: setup_inputs(seed, part) draws one part's arguments, and reference() takes and returns one part's arrays. A program takes and returns all parts, laid end to end along the dimension named above; an argument that names none is the same for every part. Nothing has to cross between parts.
Inputs may be any that keep to these rules, and one draw needn't show every extreme that they name: `courant_squared`: both fields' rows of the same model cell hold the same value. `source_cells`: row 0 is an x cell below 128, row 1 a y cell below 96, row 2 a z cell below 128. `receiver_cells`: row 0 is an x cell below 128, row 1 a y cell below 96, row 2 a z cell below 128. `snapshot_steps`: column 0 lies in 1 to 2, column 1 in 3 to 4.
All inputs are finite; a program needn't handle non-finite values.
Results may differ from the reference program's by a relative error of at most 0.0003.
Values sent between devices are 32-bit elements; how exact they have to be, the bound alone decides.
A program may use at most 64 MiB of HBM per device.

```python
import jax
import jax.numpy as jnp
from jax import lax

STEPS = 4
NSRC = 8
NREC = 256
LAGS = 17
LAGMAX = 8
NX = 128
NY = 96
NZ = 128


def place_positions(key, count):
    subkeys = jax.random.split(key, 4)
    columns = []
    for number, extent in enumerate((NX, NY, NZ)):
        drawn = jax.random.randint(subkeys[number], (count,), 0, extent)
        ranking = jax.random.permutation(jax.random.fold_in(subkeys[3], number), count)
        drawn = jnp.where(ranking == 0, extent - 1, jnp.where(ranking == 1, 0, drawn))
        columns.append(drawn)
    return jnp.stack(columns).astype(jnp.int32)


def draw_source_cells(key, part):
    return place_positions(jax.random.fold_in(key, 11), NSRC)


def draw_receiver_cells(key, part):
    return place_positions(jax.random.fold_in(key, 12), NREC)


def draw_courant_squared(key, part):
    uniform_draw = jax.random.uniform(jax.random.fold_in(key, 13), (NX, NY, NZ), jnp.float32)
    values = 0.05 + 0.13 * uniform_draw
    return jnp.concatenate([values[NX // 2:], values, values[:NX // 2]], axis=0).astype(jnp.float32)


def draw_snapshot_steps(key, part):
    subkeys = jax.random.split(jax.random.fold_in(key, 14), 4)
    early = jax.random.randint(subkeys[0], (2,), 1, STEPS // 2 + 1)
    later = jax.random.randint(subkeys[1], (2,), STEPS // 2 + 1, STEPS + 1)
    early_row = jax.random.randint(subkeys[2], (), 0, 2)
    later_row = jax.random.randint(subkeys[3], (), 0, 2)
    rows = jnp.arange(2)
    early = jnp.where(rows == early_row, 1, early)
    later = jnp.where(rows == later_row, STEPS, later)
    return jnp.stack([early, later], axis=1).astype(jnp.int32)


def draw_lag_offsets(key, part):
    subkeys = jax.random.split(jax.random.fold_in(key, 15), 2)
    values = jax.random.randint(subkeys[0], (LAGS,), -LAGMAX, LAGMAX + 1)
    ranking = jax.random.permutation(subkeys[1], LAGS)
    values = jnp.where(ranking == 0, -LAGMAX, jnp.where(ranking == 1, LAGMAX, values))
    return values.astype(jnp.int32)


def level_of(own_key, dims, cuts, low, high):
    level, own = 1.0, jax.random.fold_in(own_key, 6)
    for axis_at, shards_of in cuts:
        heights = jnp.exp(jax.random.uniform(jax.random.fold_in(own, axis_at), (shards_of,), jnp.float32, low / len(cuts), high / len(cuts)))
        level = level * jnp.repeat(heights, dims[axis_at] // shards_of).reshape([-1 if axis == axis_at else 1 for axis in range(len(dims))])
    return level


def noise(stream_key, dims, deviation, limit, cuts=(), dtype=jnp.bfloat16):
    values = deviation * jax.random.normal(stream_key, dims, jnp.float32)
    if cuts:
        values = values * level_of(stream_key, dims, cuts, -0.22, 0.18)
    return jnp.clip(values, -limit, limit).astype(dtype)


def setup_inputs(seed: int = 0, part: int = 0) -> dict:
    seeds = jax.random.split(jax.random.key(seed), 10)
    part_splits = jax.random.split(jax.random.fold_in(seeds[9], part), 10)
    return {
        "field_now": noise(part_splits[0], (2 * NX, NY, NZ), 1.0, 6.0, ((0, 8), (1, 2)), jnp.float32),
        "field_prev": noise(part_splits[1], (2 * NX, NY, NZ), 1.0, 6.0, ((0, 8), (1, 2)), jnp.float32),
        "courant_squared": draw_courant_squared(jax.random.fold_in(seeds[9], 71), part),
        "source_cells": draw_source_cells(jax.random.fold_in(jax.random.fold_in(seeds[9], part), 71), part),
        "source_wave": noise(part_splits[4], (STEPS, NSRC), 2.0, 8.0, (), jnp.float32),
        "receiver_cells": draw_receiver_cells(jax.random.fold_in(jax.random.fold_in(seeds[9], part), 71), part),
        "receiver_wave": noise(part_splits[6], (STEPS, NREC), 2.0, 8.0, (), jnp.float32),
        "snapshot_steps": draw_snapshot_steps(jax.random.fold_in(jax.random.fold_in(seeds[9], part), 71), part),
        "lag_offsets": draw_lag_offsets(jax.random.fold_in(seeds[9], 71), part),
    }


centre_weight = -205.0 / 72.0
stencil_weights = (1.6, -0.2, 8.0 / 315.0, -1.0 / 560.0)


def laplace_padded(padded, count_x, count_y, count_z):
    def window(shift_x, shift_y, shift_z):
        return padded[4 + shift_x:4 + shift_x + count_x, 4 + shift_y:4 + shift_y + count_y, 4 + shift_z:4 + shift_z + count_z]

    result = (3.0 * centre_weight) * window(0, 0, 0)
    for offset, weight in enumerate(stencil_weights, 1):
        paired = window(offset, 0, 0) + window(-offset, 0, 0)
        paired = paired + window(0, offset, 0) + window(0, -offset, 0)
        paired = paired + window(0, 0, offset) + window(0, 0, -offset)
        result = result + weight * paired
    return result


def march(current, previous, courant_half, positions, amounts, wanted):
    held = [jnp.zeros_like(current), jnp.zeros_like(current)]
    for number in range(STEPS):
        padded = jnp.pad(current, 4)
        advanced = 2.0 * current - previous + courant_half * laplace_padded(padded, NX, NY, NZ)
        advanced = advanced.at[positions[0], positions[1], positions[2]].add(amounts[number])
        held = [jnp.where(wanted[snapshot_slot] == number + 1, advanced, held[snapshot_slot]) for snapshot_slot in range(2)]
        previous, current = current, advanced
    return current, held


def source_rows(array):
    return array[NX // 2:NX // 2 + NX]


def receiver_rows(array):
    return jnp.concatenate([array[NX // 2 + NX:], array[:NX // 2]], axis=0)


def lag_products(source_even, receiver_even, lag_offsets, z_first, z_count):
    pad_width = ((0, 0), (0, 0), (LAGMAX, LAGMAX))
    source_pad = jnp.pad(source_even, pad_width)
    receiver_pad = jnp.pad(receiver_even, pad_width)

    def one_lag(offset):
        start_source = (z_first + LAGMAX - offset).astype(jnp.int32)
        start_receiver = (z_first + LAGMAX + offset).astype(jnp.int32)
        shifted_source = lax.dynamic_slice_in_dim(source_pad, start_source, 2 * z_count, 2)[:, :, ::2]
        shifted_receiver = lax.dynamic_slice_in_dim(receiver_pad, start_receiver, 2 * z_count, 2)[:, :, ::2]
        return shifted_source * shifted_receiver

    return lax.map(one_lag, lag_offsets)


def reference(field_now, field_prev, courant_squared, source_cells, source_wave, receiver_cells, receiver_wave, snapshot_steps, lag_offsets):
    source_final, source_held = march(source_rows(field_now), source_rows(field_prev), source_rows(courant_squared), source_cells, source_wave, snapshot_steps[0])
    receiver_final, receiver_held = march(receiver_rows(field_now), receiver_rows(field_prev), receiver_rows(courant_squared), receiver_cells, receiver_wave, snapshot_steps[1])
    final_field = jnp.concatenate([receiver_final[NX // 2:], source_final, receiver_final[:NX // 2]], axis=0)
    extended = lag_products(source_held[0][::2, ::2, :], receiver_held[0][::2, ::2, :], lag_offsets, 0, NZ // 2)
    extended = extended + lag_products(source_held[1][::2, ::2, :], receiver_held[1][::2, ::2, :], lag_offsets, 0, NZ // 2)
    quarter = NZ // 4
    upper_part = jnp.transpose(extended[:, :, :, :quarter], (1, 0, 2, 3)).reshape(NX // 2, LAGS, (NY // 2) * quarter)
    lower_part = jnp.transpose(extended[:, :, :, quarter:], (1, 0, 2, 3)).reshape(NX // 2, LAGS, (NY // 2) * quarter)
    extended_image = jnp.concatenate([lower_part[NX // 4:], upper_part, lower_part[:NX // 4]], axis=0)
    return final_field, extended_image
```

```python
import functools

import jax
import jax.numpy as jnp
from jax import lax
from jax.experimental import pallas as pl
from jax.experimental.pallas import tpu as pltpu
from jax.sharding import PartitionSpec as P

STEPS = 4
WIDTH = 4
GROUP = 4
ROW = 8
centre_weight = -205.0 / 72.0
stencil_weights = (1.6, -0.2, 8.0 / 315.0, -1.0 / 560.0)
MESH = pl.DeviceIdType.MESH
f32, bf16 = jnp.float32, jnp.bfloat16


def halves(value):
    high = value.astype(bf16)
    low = (value - high.astype(f32)).astype(bf16)
    return high, low


def kernel(
    now_ref, prev_ref, courant_ref, scell_ref, swave_ref, rcell_ref, rwave_ref, steps_ref, lag_ref,
    final_ref, image_ref,
    fields, courant, band, inject, choose_own, choose_other, snap, other, x_own, x_other, cells, waves,
    x_send, x_recv, y_send, y_recv, t_send, t_recv, local,
):
    nx, ny, nz = now_ref.shape
    lags = lag_ref.shape[0]
    points = cells.shape[1]
    loop = lax.axis_size("gx")
    half = loop // 2
    turn = loop // 4
    gx = lax.axis_index("gx")
    gy = lax.axis_index("gy")
    relative = lax.rem(gx - turn + loop, loop)
    which = relative // half
    slab = lax.rem(relative, half)
    low_id = {"gx": lax.rem(gx - 1 + loop, loop)}
    high_id = {"gx": lax.rem(gx + 1, loop)}
    peer_id = {"gy": 1 - gy}
    trade_id = {"gx": lax.rem(gx + half, loop)}
    has_low = slab > 0
    has_high = slab < half - 1
    y_src = pl.multiple_of(jnp.where(gy == 0, ny, ROW), ROW)
    y_src0 = pl.multiple_of(jnp.where(gy == 0, ny - ROW, 0), ROW)
    y_dst = pl.multiple_of(jnp.where(gy == 0, 0, ny + ROW), ROW)

    inner = (pl.ds(WIDTH, nx), pl.ds(ROW, ny))
    loads = [
        pltpu.make_async_copy(now_ref, fields.at[0, inner[0], inner[1]], local.at[0]),
        pltpu.make_async_copy(prev_ref, fields.at[1, inner[0], inner[1]], local.at[1]),
        pltpu.make_async_copy(courant_ref, courant, local.at[2]),
    ]
    for load in loads:
        load.start()

    for parity in range(2):
        edge = jnp.zeros((WIDTH, ny + 2 * ROW, nz), f32)
        fields[parity, 0:WIDTH] = edge
        fields[parity, WIDTH + nx:] = edge
        side = jnp.zeros((nx, ROW, nz), f32)
        fields[parity, WIDTH:WIDTH + nx, 0:ROW] = side
        fields[parity, WIDTH:WIDTH + nx, ROW + ny:] = side

    barrier = pltpu.get_barrier_semaphore()
    pl.semaphore_signal(barrier, inc=1, device_id=peer_id, device_id_type=MESH)
    pl.semaphore_signal(barrier, inc=1, device_id=trade_id, device_id_type=MESH)

    @pl.when(has_low)
    def _():
        pl.semaphore_signal(barrier, inc=1, device_id=low_id, device_id_type=MESH)

    @pl.when(has_high)
    def _():
        pl.semaphore_signal(barrier, inc=1, device_id=high_id, device_id_type=MESH)

    pl.semaphore_wait(barrier, 2 + has_low.astype(jnp.int32) + has_high.astype(jnp.int32))

    rows = pl.ds(ROW, ny)

    def x_copy(s, way):
        at = s % 2
        if s == 0:
            src = now_ref.at[pl.ds(0 if way == 0 else nx - WIDTH, WIDTH)]
        else:
            src = fields.at[at, pl.ds(WIDTH if way == 0 else nx, WIDTH), rows]
        return pltpu.make_async_remote_copy(
            src_ref=src,
            dst_ref=fields.at[at, pl.ds(WIDTH + nx if way == 0 else 0, WIDTH), rows],
            send_sem=x_send.at[s, way],
            recv_sem=x_recv.at[s, way],
            device_id=low_id if way == 0 else high_id,
            device_id_type=MESH,
        )

    parts = ((GROUP, nx - 2 * GROUP), (0, GROUP), (nx - GROUP, GROUP))

    def y_copy(s, part):
        at = s % 2
        begin, size = parts[part]
        if s == 0:
            src = now_ref.at[pl.ds(begin, size), pl.ds(y_src0, ROW)]
        else:
            src = fields.at[at, pl.ds(WIDTH + begin, size), pl.ds(y_src, ROW)]
        return pltpu.make_async_remote_copy(
            src_ref=src,
            dst_ref=fields.at[at, pl.ds(WIDTH + begin, size), pl.ds(y_dst, ROW)],
            send_sem=y_send.at[s, part],
            recv_sem=y_recv.at[s, part],
            device_id=peer_id,
            device_id_type=MESH,
        )

    def trade(k):
        return pltpu.make_async_remote_copy(
            src_ref=snap.at[k],
            dst_ref=other.at[k],
            send_sem=t_send.at[k],
            recv_sem=t_recv.at[k],
            device_id=trade_id,
            device_id_type=MESH,
        )

    def x_start(s):
        @pl.when(has_low)
        def _():
            x_copy(s, 0).start()

        @pl.when(has_high)
        def _():
            x_copy(s, 1).start()

    def x_arrived(s):
        @pl.when(has_high)
        def _():
            x_copy(s, 0).wait_recv()

        @pl.when(has_low)
        def _():
            x_copy(s, 1).wait_recv()

    def x_left(s):
        @pl.when(has_low)
        def _():
            x_copy(s, 0).wait_send()

        @pl.when(has_high)
        def _():
            x_copy(s, 1).wait_send()

    x_start(0)
    for part in range(3):
        y_copy(0, part).start()

    apart = jnp.abs(
        lax.broadcasted_iota(jnp.int32, (nz, nz), 0) - lax.broadcasted_iota(jnp.int32, (nz, nz), 1)
    )
    matrix = jnp.where(apart == 0, f32(3.0 * centre_weight), f32(0.0))
    for k, weight in enumerate(stencil_weights, 1):
        matrix = jnp.where(apart == k, f32(weight), matrix)
    matrix_high, matrix_low = halves(matrix)
    band[0:nz] = matrix_high
    band[nz:2 * nz] = matrix_high
    band[2 * nz:] = matrix_low

    is_source = which == 0
    count = scell_ref.shape[1]
    cells[...] = jnp.full(cells.shape, -1, jnp.int32)
    waves[...] = jnp.zeros(waves.shape, f32)
    cells[0:3, 0:count] = scell_ref[...]
    waves[0:STEPS, 0:count] = swave_ref[...]
    cell = jnp.where(is_source, cells[0:3], rcell_ref[...])
    wave = jnp.where(is_source, waves[0:STEPS], rwave_ref[...])
    at_x = cell[0:1] - slab * nx
    at_y = cell[1:2] - gy * ny
    inside = (at_x >= 0) & (at_x < nx) & (at_y >= 0) & (at_y < ny)
    line = jnp.where(inside, at_x * ny + at_y, -1)
    at_z = lax.broadcasted_iota(jnp.int32, (nz, points), 0) == cell[2:3]
    amounts = []
    for s in range(STEPS):
        high, low = halves(jnp.where(at_z, wave[s:s + 1], 0.0))
        amounts.append(jnp.concatenate([high, low], axis=1))
    amounts = jnp.concatenate(amounts, axis=0)
    chunk = GROUP * ny

    def spread(g, carry):
        row = lax.broadcasted_iota(jnp.int32, (chunk, points), 0) + g * chunk
        hit = jnp.where(row == line, f32(1.0), f32(0.0)).astype(bf16)
        hit = jnp.concatenate([hit, hit], axis=1)
        added = lax.dot_general(
            hit, amounts, (((1,), (1,)), ((), ())), preferred_element_type=f32
        )
        for s in range(STEPS):
            inject[s, pl.ds(pl.multiple_of(g * chunk, chunk), chunk), :] = added[:, s * nz:(s + 1) * nz]
        return carry

    lax.fori_loop(0, nx // GROUP, spread, 0)

    quarter = nz // 4
    lane = lax.broadcasted_iota(jnp.int32, (nz, nz), 1)
    depth = lax.broadcasted_iota(jnp.int32, (nz, nz), 0)
    twice = 2 * (which * quarter + lax.rem(lane, quarter)) - depth
    spot = lane // quarter
    sign = jnp.where(is_source, -1, 1)
    far = 4 * nz

    def choose(h, carry):
        lag = lag_ref[h] * sign
        for r in range(4):
            mine = jnp.where(spot == r, twice, far)
            choose_own[h, r * nz:(r + 1) * nz, :] = jnp.where(mine == -lag, f32(1.0), f32(0.0)).astype(bf16)
            choose_other[h, r * nz:(r + 1) * nz, :] = jnp.where(mine == lag, f32(1.0), f32(0.0)).astype(bf16)
        return carry

    lax.fori_loop(0, lags, choose, 0)

    for load in loads:
        load.wait()

    def group(s, g):
        a, b = (s - 1) % 2, s % 2
        base = WIDTH + g * GROUP
        centre = fields[a, pl.ds(base, GROUP), rows, :].reshape(GROUP * ny, nz)
        high, low = halves(centre)
        along = jnp.dot(
            jnp.concatenate([high, low, high], axis=1), band[...], preferred_element_type=f32
        )
        for i in range(GROUP):
            x = base + i
            total = along[i * ny:(i + 1) * ny]
            for k, weight in enumerate(stencil_weights, 1):
                pair = fields[a, x + k, rows, :] + fields[a, x - k, rows, :]
                pair = pair + fields[a, x, pl.ds(ROW + k, ny), :] + fields[a, x, pl.ds(ROW - k, ny), :]
                total = total + weight * pair
            at = g * GROUP + i
            fields[b, x, rows, :] = (
                2.0 * fields[a, x, rows, :]
                - fields[b, x, rows, :]
                + courant[at] * total
                + inject[s - 1, pl.ds(pl.multiple_of(at * ny, ny), ny), :]
            )

    def hold(k, wanted):
        def one(i, carry):
            for r in range(4):
                cut = pl.ds(ROW + 2 * r, ny // ROW, ROW)
                early = fields[1, WIDTH + 2 * i, cut, :]
                late = fields[0, WIDTH + 2 * i, cut, :]
                snap[k, r, pl.ds(i, ny // ROW, nx // 2), :] = jnp.where(wanted == 2 * k + 1, early, late)
            return carry

        lax.fori_loop(0, nx // 2, one, 0)

    def split(ref, k, to):
        count = ref.shape[2]
        for r in range(4):
            high, low = halves(ref[k, r])
            to[0:count, r * nz:(r + 1) * nz] = high
            to[count:, r * nz:(r + 1) * nz] = low

    def image(k):
        split(snap, k, x_own)
        trade(k).wait_recv()
        split(other, k, x_other)
        count = snap.shape[2]

        def one(h, carry):
            mine = jnp.dot(x_own[...], choose_own[h], preferred_element_type=f32)
            theirs = jnp.dot(x_other[...], choose_other[h], preferred_element_type=f32)
            value = (mine[:count] + mine[count:]) * (theirs[:count] + theirs[count:])
            place = pl.ds(h, count, image_ref.shape[0] // count)
            if k == 0:
                image_ref[place, :] = value
            else:
                image_ref[place, :] = image_ref[place, :] + value
            return carry

        lax.fori_loop(0, lags, one, 0)

    groups = nx // GROUP
    for s in range(1, STEPS + 1):
        y_copy(s - 1, 0).wait_recv()
        if s >= 2:
            x_left(s - 2)
            for part in range(3):
                y_copy(s - 2, part).wait_send()

        def inside_group(g, carry):
            group(s, g)
            return carry

        def rim_group(i, carry):
            group(s, i * (groups - 1))
            return carry

        lax.fori_loop(1, groups - 1, inside_group, 0)
        if s < STEPS:
            y_copy(s, 0).start()
        x_arrived(s - 1)
        y_copy(s - 1, 1).wait_recv()
        y_copy(s - 1, 2).wait_recv()
        lax.fori_loop(0, 2, rim_group, 0)
        if s < STEPS:
            x_start(s)
            y_copy(s, 1).start()
            y_copy(s, 2).start()
        if s % 2 == 0:
            k = s // 2 - 1
            hold(k, steps_ref[which, k])
            trade(k).start()
    store = pltpu.make_async_copy(fields.at[STEPS % 2, inner[0], inner[1]], final_ref, local.at[3])
    store.start()
    x_left(STEPS - 1)
    for part in range(3):
        y_copy(STEPS - 1, part).wait_send()
    image(0)
    image(1)
    trade(0).wait_send()
    trade(1).wait_send()
    store.wait()


def body(now, prev, courant, source_cells, source_wave, receiver_cells, receiver_wave, steps, lag_offsets):
    nx, ny, nz = now.shape
    lags = lag_offsets.shape[0]
    deep = -(-lags // 8) * 8
    packed = (nx // 2) * (ny // 8)
    points = receiver_cells.shape[1]
    vmem = pl.BlockSpec(memory_space=pltpu.VMEM)
    smem = pl.BlockSpec(memory_space=pltpu.SMEM)
    anywhere = pl.BlockSpec(memory_space=pl.ANY)
    dma = pltpu.SemaphoreType.DMA
    final, image = pl.pallas_call(
        kernel,
        out_shape=(
            jax.ShapeDtypeStruct(now.shape, f32),
            jax.ShapeDtypeStruct((packed * deep, nz), f32),
        ),
        in_specs=[anywhere] * 3 + [vmem] * 4 + [smem] * 2,
        out_specs=(anywhere, vmem),
        scratch_shapes=[
            pltpu.VMEM((2, nx + 2 * WIDTH, ny + 2 * ROW, nz), f32),
            pltpu.VMEM((nx, ny, nz), f32),
            pltpu.VMEM((3 * nz, nz), bf16),
            pltpu.VMEM((STEPS, nx * ny, nz), f32),
            pltpu.VMEM((lags, 4 * nz, nz), bf16),
            pltpu.VMEM((lags, 4 * nz, nz), bf16),
            pltpu.VMEM((2, 4, packed, nz), f32),
            pltpu.VMEM((2, 4, packed, nz), f32),
            pltpu.VMEM((2 * packed, 4 * nz), bf16),
            pltpu.VMEM((2 * packed, 4 * nz), bf16),
            pltpu.VMEM((8, points), jnp.int32),
            pltpu.VMEM((8, points), f32),
            dma((STEPS, 2)),
            dma((STEPS, 2)),
            dma((STEPS, 3)),
            dma((STEPS, 3)),
            dma((2,)),
            dma((2,)),
            dma((4,)),
        ],
        compiler_params=pltpu.CompilerParams(
            collective_id=0, has_side_effects=True, vmem_limit_bytes=48 * 1024 * 1024
        ),
    )(now, prev, courant, source_cells, source_wave, receiver_cells, receiver_wave, steps, lag_offsets)
    image = image.reshape(ny // 8, nx // 2, deep, nz)[:, :, :lags]
    image = jnp.transpose(image, (1, 2, 0, 3)).reshape(nx // 2, lags, (ny // 8) * nz)
    return final, image


def solution(mesh):
    placed = (
        P(("shots", "gx"), "gy", None),
        P(("shots", "gx"), "gy", None),
        P("gx", "gy", None),
        P(None, "shots"),
        P(None, "shots"),
        P(None, "shots"),
        P(None, "shots"),
        P("shots", None),
        P(),
    )
    return jax.shard_map(
        body,
        mesh=mesh,
        in_specs=placed,
        out_specs=(P(("shots", "gx"), "gy", None), P(("shots", "gx"), None, "gy")),
        check_vma=False,
    )
```

```python
import functools

import jax
import jax.numpy as jnp
from jax import lax
from jax.experimental import pallas as pl
from jax.experimental.pallas import tpu as pltpu
from jax.sharding import PartitionSpec as P

STEPS = 4
WIDTH = 4
GROUP = 4
ROW = 8
centre_weight = -205.0 / 72.0
stencil_weights = (1.6, -0.2, 8.0 / 315.0, -1.0 / 560.0)
MESH = pl.DeviceIdType.MESH
f32, bf16 = jnp.float32, jnp.bfloat16


def halves(value):
    high = value.astype(bf16)
    low = (value - high.astype(f32)).astype(bf16)
    return high, low


def kernel(
    now_ref, prev_ref, courant_ref, scell_in, swave_in, rcell_in, rwave_in, steps_in, lag_in,
    final_ref, image_ref,
    scell_ref, swave_ref, rcell_ref, rwave_ref, steps_ref, lag_ref,
    fields, courant, band, inject, choose_own, choose_other, snap, sent, other, x_own, x_other, total_ref, cells, waves,
    x_send, x_recv, y_send, y_recv, t_send, t_recv, local,
):
    nx, ny, nz = now_ref.shape
    lags = lag_ref.shape[0]
    points = cells.shape[1]
    loop = lax.axis_size("gx")
    half = loop // 2
    turn = loop // 4
    gx = lax.axis_index("gx")
    gy = lax.axis_index("gy")
    relative = lax.rem(gx - turn + loop, loop)
    which = relative // half
    slab = lax.rem(relative, half)
    low_id = {"gx": lax.rem(gx - 1 + loop, loop)}
    high_id = {"gx": lax.rem(gx + 1, loop)}
    peer_id = {"gy": 1 - gy}
    trade_id = {"gx": lax.rem(gx + half, loop)}
    has_low = slab > 0
    has_high = slab < half - 1
    y_src = pl.multiple_of(jnp.where(gy == 0, ny, ROW), ROW)
    y_src0 = pl.multiple_of(jnp.where(gy == 0, ny - ROW, 0), ROW)
    y_dst = pl.multiple_of(jnp.where(gy == 0, 0, ny + ROW), ROW)

    inner = (pl.ds(WIDTH, nx), pl.ds(ROW, ny))
    loads = [
        pltpu.make_async_copy(now_ref, fields.at[0, inner[0], inner[1]], local.at[0]),
        pltpu.make_async_copy(prev_ref, fields.at[1, inner[0], inner[1]], local.at[1]),
        pltpu.make_async_copy(courant_ref, courant, local.at[2]),
    ]
    small = (
        (scell_in, scell_ref), (swave_in, swave_ref), (rcell_in, rcell_ref),
        (rwave_in, rwave_ref), (steps_in, steps_ref), (lag_in, lag_ref),
    )
    tables = [
        pltpu.make_async_copy(src, dst, local.at[4 + i]) for i, (src, dst) in enumerate(small)
    ]
    for load in tables + loads:
        load.start()

    for parity in range(2):
        edge = jnp.zeros((WIDTH, ny + 2 * ROW, nz), f32)
        fields[parity, 0:WIDTH] = edge
        fields[parity, WIDTH + nx:] = edge
        side = jnp.zeros((nx, ROW, nz), f32)
        fields[parity, WIDTH:WIDTH + nx, 0:ROW] = side
        fields[parity, WIDTH:WIDTH + nx, ROW + ny:] = side

    barrier = pltpu.get_barrier_semaphore()
    pl.semaphore_signal(barrier, inc=1, device_id=peer_id, device_id_type=MESH)
    pl.semaphore_signal(barrier, inc=1, device_id=trade_id, device_id_type=MESH)

    @pl.when(has_low)
    def _():
        pl.semaphore_signal(barrier, inc=1, device_id=low_id, device_id_type=MESH)

    @pl.when(has_high)
    def _():
        pl.semaphore_signal(barrier, inc=1, device_id=high_id, device_id_type=MESH)

    pl.semaphore_wait(barrier, 2 + has_low.astype(jnp.int32) + has_high.astype(jnp.int32))

    rows = pl.ds(ROW, ny)

    def x_copy(s, way):
        at = s % 2
        if s == 0:
            src = now_ref.at[pl.ds(0 if way == 0 else nx - WIDTH, WIDTH)]
        else:
            src = fields.at[at, pl.ds(WIDTH if way == 0 else nx, WIDTH), rows]
        return pltpu.make_async_remote_copy(
            src_ref=src,
            dst_ref=fields.at[at, pl.ds(WIDTH + nx if way == 0 else 0, WIDTH), rows],
            send_sem=x_send.at[s, way],
            recv_sem=x_recv.at[s, way],
            device_id=low_id if way == 0 else high_id,
            device_id_type=MESH,
        )

    parts = ((GROUP, nx - 2 * GROUP), (0, GROUP), (nx - GROUP, GROUP))

    def y_copy(s, part):
        at = s % 2
        begin, size = parts[part]
        if s == 0:
            src = now_ref.at[pl.ds(begin, size), pl.ds(y_src0, ROW)]
        else:
            src = fields.at[at, pl.ds(WIDTH + begin, size), pl.ds(y_src, ROW)]
        return pltpu.make_async_remote_copy(
            src_ref=src,
            dst_ref=fields.at[at, pl.ds(WIDTH + begin, size), pl.ds(y_dst, ROW)],
            send_sem=y_send.at[s, part],
            recv_sem=y_recv.at[s, part],
            device_id=peer_id,
            device_id_type=MESH,
        )

    def trade(k):
        return pltpu.make_async_remote_copy(
            src_ref=sent.at[k],
            dst_ref=other.at[k],
            send_sem=t_send.at[k],
            recv_sem=t_recv.at[k],
            device_id=trade_id,
            device_id_type=MESH,
        )

    def x_start(s):
        @pl.when(has_low)
        def _():
            x_copy(s, 0).start()

        @pl.when(has_high)
        def _():
            x_copy(s, 1).start()

    def x_arrived(s):
        @pl.when(has_high)
        def _():
            x_copy(s, 0).wait_recv()

        @pl.when(has_low)
        def _():
            x_copy(s, 1).wait_recv()

    def x_left(s):
        @pl.when(has_low)
        def _():
            x_copy(s, 0).wait_send()

        @pl.when(has_high)
        def _():
            x_copy(s, 1).wait_send()

    x_start(0)
    for part in range(3):
        y_copy(0, part).start()

    apart = jnp.abs(
        lax.broadcasted_iota(jnp.int32, (nz, nz), 0) - lax.broadcasted_iota(jnp.int32, (nz, nz), 1)
    )
    matrix = jnp.where(apart == 0, f32(3.0 * centre_weight), f32(0.0))
    for k, weight in enumerate(stencil_weights, 1):
        matrix = jnp.where(apart == k, f32(weight), matrix)
    matrix_high, matrix_low = halves(matrix)
    band[0:nz] = matrix_high
    band[nz:2 * nz] = matrix_high
    band[2 * nz:] = matrix_low

    for load in tables:
        load.wait()
    is_source = which == 0
    count = scell_ref.shape[1]
    cells[...] = jnp.full(cells.shape, -1, jnp.int32)
    waves[...] = jnp.zeros(waves.shape, f32)
    cells[0:3, 0:count] = scell_ref[...]
    waves[0:STEPS, 0:count] = swave_ref[...]
    cell = jnp.where(is_source, cells[0:3], rcell_ref[...])
    wave = jnp.where(is_source, waves[0:STEPS], rwave_ref[...])
    at_x = cell[0:1] - slab * nx
    at_y = cell[1:2] - gy * ny
    inside = (at_x >= 0) & (at_x < nx) & (at_y >= 0) & (at_y < ny)
    line = jnp.where(inside, at_x * ny + at_y, -1)
    at_z = lax.broadcasted_iota(jnp.int32, (nz, points), 0) == cell[2:3]
    amounts = []
    for s in range(STEPS):
        high, low = halves(jnp.where(at_z, wave[s:s + 1], 0.0))
        amounts.append(jnp.concatenate([high, low], axis=1))
    amounts = jnp.concatenate(amounts, axis=0)
    chunk = GROUP * ny

    def spread(g, carry):
        row = lax.broadcasted_iota(jnp.int32, (chunk, points), 0) + g * chunk
        hit = jnp.where(row == line, f32(1.0), f32(0.0)).astype(bf16)
        hit = jnp.concatenate([hit, hit], axis=1)
        added = lax.dot_general(
            hit, amounts, (((1,), (1,)), ((), ())), preferred_element_type=f32
        )
        for s in range(STEPS):
            inject[s, pl.ds(pl.multiple_of(g * chunk, chunk), chunk), :] = added[:, s * nz:(s + 1) * nz]
        return carry

    lax.fori_loop(0, nx // GROUP, spread, 0)

    quarter = nz // 4
    middle = nz // 2
    lane = lax.broadcasted_iota(jnp.int32, (nz, nz), 1)
    depth = lax.broadcasted_iota(jnp.int32, (nz, nz), 0)
    twice = 2 * (which * quarter + lax.rem(lane, quarter)) - depth
    spot = lane // quarter
    sign = jnp.where(is_source, -1, 1)
    far = 4 * nz
    sets = -(-lags // 4)
    for g in range(sets):
        lag = jnp.full((nz, nz), far, jnp.int32)
        for i in range(min(4, lags - 4 * g)):
            lag = jnp.where(spot == i, lag_ref[4 * g + i] * sign, lag)
        for ref, hit in ((choose_own, twice == -lag), (choose_other, twice == lag)):
            one = jnp.where(hit, f32(1.0), f32(0.0)).astype(bf16)
            ref[g, 0:nz, :] = one
            ref[g, nz:, :] = one

    for load in loads:
        load.wait()

    def group(s, g):
        a, b = (s - 1) % 2, s % 2
        base = WIDTH + g * GROUP
        centre = fields[a, pl.ds(base, GROUP), rows, :].reshape(GROUP * ny, nz)
        high, low = halves(centre)
        along = jnp.dot(
            jnp.concatenate([high, low, high], axis=1), band[...], preferred_element_type=f32
        )
        for i in range(GROUP):
            x = base + i
            total = along[i * ny:(i + 1) * ny]
            for k, weight in enumerate(stencil_weights, 1):
                pair = fields[a, x + k, rows, :] + fields[a, x - k, rows, :]
                pair = pair + fields[a, x, pl.ds(ROW + k, ny), :] + fields[a, x, pl.ds(ROW - k, ny), :]
                total = total + weight * pair
            at = g * GROUP + i
            fields[b, x, rows, :] = (
                2.0 * fields[a, x, rows, :]
                - fields[b, x, rows, :]
                + courant[at] * total
                + inject[s - 1, pl.ds(pl.multiple_of(at * ny, ny), ny), :]
            )

    def hold(k, wanted):
        def one(i, carry):
            for r in range(4):
                cut = pl.ds(ROW + 2 * r, ny // ROW, ROW)
                early = fields[1, WIDTH + 2 * i, cut, :]
                late = fields[0, WIDTH + 2 * i, cut, :]
                snap[k, r, pl.ds(i, ny // ROW, nx // 2), :] = jnp.where(wanted == 2 * k + 1, early, late)
            return carry

        lax.fori_loop(0, nx // 2, one, 0)

    packed = snap.shape[2]
    part_rows = packed // 4
    edge_row = 2 * packed

    def pack(k):
        place = lax.broadcasted_iota(jnp.int32, (packed, nz), 1)
        strip = lax.broadcasted_iota(jnp.int32, (part_rows, nz), 1) // ROW
        for pair in range(2):
            even, odd = snap[k, 2 * pair], snap[k, 2 * pair + 1]
            first = jnp.where(is_source, pltpu.roll(even, middle, 1), even)
            second = jnp.where(is_source, odd, pltpu.roll(odd, middle, 1))
            sent[k, pair * packed:(pair + 1) * packed, :] = jnp.where(place < middle, first, second)
        edge = jnp.zeros((part_rows, nz), f32)
        for r in range(4):
            plane = snap[k, r]
            plane = jnp.where(is_source, pltpu.roll(plane, ROW, 1), plane)
            for j in range(4):
                slot = 4 * r + j
                piece = plane[j * part_rows:(j + 1) * part_rows]
                by = (slot * ROW - middle) % nz
                piece = pltpu.roll(piece, by, 1) if by else piece
                edge = jnp.where(strip == slot, piece, edge)
        sent[k, edge_row:, :] = edge

    def unpack(k):
        place = lax.broadcasted_iota(jnp.int32, (packed, nz), 1)
        main = jnp.where(is_source, place, nz - 1 - place) < middle
        from_edge = jnp.where(is_source, middle, middle - ROW)
        near = (place >= from_edge) & (place < from_edge + ROW)
        edge = other[k, edge_row:, :]
        for r in range(4):
            pair = r // 2
            straight = other[k, pair * packed:(pair + 1) * packed, :]
            turned = pltpu.roll(straight, middle, 1)
            if r % 2 == 0:
                body_part = jnp.where(is_source, straight, turned)
            else:
                body_part = jnp.where(is_source, turned, straight)
            pieces = []
            for j in range(4):
                by = (middle - (4 * r + j) * ROW) % nz
                pieces.append(pltpu.roll(edge, by, 1) if by else edge)
            rim = jnp.concatenate(pieces, axis=0)
            rim = jnp.where(is_source, rim, pltpu.roll(rim, nz - ROW, 1))
            high, low = halves(jnp.where(main, body_part, jnp.where(near, rim, 0.0)))
            x_other[r * packed:(r + 1) * packed, 0:nz] = high
            x_other[r * packed:(r + 1) * packed, nz:] = low

    def image(k):
        for r in range(4):
            high, low = halves(snap[k, r])
            x_own[r * packed:(r + 1) * packed, 0:nz] = high
            x_own[r * packed:(r + 1) * packed, nz:] = low
        trade(k).wait_recv()
        unpack(k)
        field_of = lax.broadcasted_iota(jnp.int32, (packed, nz), 1) // quarter
        for g in range(sets):
            mine = jnp.dot(x_own[...], choose_own[g], preferred_element_type=f32)
            theirs = jnp.dot(x_other[...], choose_other[g], preferred_element_type=f32)
            if k == 0:
                total_ref[g] = mine * theirs
                continue
            value = total_ref[g] + mine * theirs
            turned = []
            for r in range(4):
                piece = value[r * packed:(r + 1) * packed]
                turned.append(pltpu.roll(piece, r * quarter, 1) if r else piece)
            for i in range(min(4, lags - 4 * g)):
                line = turned[0]
                for r in range(1, 4):
                    line = jnp.where(field_of == (i + r) % 4, turned[r], line)
                line = pltpu.roll(line, nz - i * quarter, 1) if i else line
                for q in range(ny // ROW):
                    image_ref[4 * g + i, :, q * nz:(q + 1) * nz] = line[q * (nx // 2):(q + 1) * (nx // 2)]

    groups = nx // GROUP
    for s in range(1, STEPS + 1):
        y_copy(s - 1, 0).wait_recv()
        if s >= 2:
            x_left(s - 2)
            for part in range(3):
                y_copy(s - 2, part).wait_send()

        def inside_group(g, carry):
            group(s, g)
            return carry

        def rim_group(i, carry):
            group(s, i * (groups - 1))
            return carry

        lax.fori_loop(1, groups - 1, inside_group, 0)
        if s < STEPS:
            y_copy(s, 0).start()
        x_arrived(s - 1)
        y_copy(s - 1, 1).wait_recv()
        y_copy(s - 1, 2).wait_recv()
        lax.fori_loop(0, 2, rim_group, 0)
        if s < STEPS:
            x_start(s)
            y_copy(s, 1).start()
            y_copy(s, 2).start()
        if s % 2 == 0:
            k = s // 2 - 1
            hold(k, steps_ref[which, k])
            pack(k)
            trade(k).start()
    store = pltpu.make_async_copy(fields.at[STEPS % 2, inner[0], inner[1]], final_ref, local.at[3])
    store.start()
    x_left(STEPS - 1)
    for part in range(3):
        y_copy(STEPS - 1, part).wait_send()
    image(0)
    image(1)
    trade(0).wait_send()
    trade(1).wait_send()
    store.wait()


def body(now, prev, courant, source_cells, source_wave, receiver_cells, receiver_wave, steps, lag_offsets):
    nx, ny, nz = now.shape
    lags = lag_offsets.shape[0]
    packed = (nx // 2) * (ny // 8)
    points = receiver_cells.shape[1]
    vmem = pl.BlockSpec(memory_space=pltpu.VMEM)
    hbm = pl.BlockSpec(memory_space=pltpu.HBM)
    dma = pltpu.SemaphoreType.DMA
    final, image = pl.pallas_call(
        kernel,
        out_shape=(
            jax.ShapeDtypeStruct(now.shape, f32),
            jax.ShapeDtypeStruct((lags, nx // 2, (ny // 8) * nz), f32),
        ),
        in_specs=[hbm] * 9,
        out_specs=(hbm, vmem),
        scratch_shapes=[
            pltpu.VMEM(source_cells.shape, jnp.int32),
            pltpu.VMEM(source_wave.shape, f32),
            pltpu.VMEM(receiver_cells.shape, jnp.int32),
            pltpu.VMEM(receiver_wave.shape, f32),
            pltpu.SMEM(steps.shape, jnp.int32),
            pltpu.SMEM(lag_offsets.shape, jnp.int32),
            pltpu.VMEM((2, nx + 2 * WIDTH, ny + 2 * ROW, nz), f32),
            pltpu.VMEM((nx, ny, nz), f32),
            pltpu.VMEM((3 * nz, nz), bf16),
            pltpu.VMEM((STEPS, nx * ny, nz), f32),
            pltpu.VMEM((-(-lags // 4), 2 * nz, nz), bf16),
            pltpu.VMEM((-(-lags // 4), 2 * nz, nz), bf16),
            pltpu.VMEM((2, 4, packed, nz), f32),
            pltpu.VMEM((2, 2 * packed + packed // 4, nz), f32),
            pltpu.VMEM((2, 2 * packed + packed // 4, nz), f32),
            pltpu.VMEM((4 * packed, 2 * nz), bf16),
            pltpu.VMEM((4 * packed, 2 * nz), bf16),
            pltpu.VMEM((-(-lags // 4), 4 * packed, nz), f32),
            pltpu.VMEM((8, points), jnp.int32),
            pltpu.VMEM((8, points), f32),
            dma((STEPS, 2)),
            dma((STEPS, 2)),
            dma((STEPS, 3)),
            dma((STEPS, 3)),
            dma((2,)),
            dma((2,)),
            dma((10,)),
        ],
        compiler_params=pltpu.CompilerParams(
            collective_id=0, has_side_effects=True, vmem_limit_bytes=62 * 1024 * 1024
        ),
    )(now, prev, courant, source_cells, source_wave, receiver_cells, receiver_wave, steps, lag_offsets)
    return final, jnp.transpose(image, (1, 0, 2))


def solution(mesh):
    placed = (
        P(("shots", "gx"), "gy", None),
        P(("shots", "gx"), "gy", None),
        P("gx", "gy", None),
        P(None, "shots"),
        P(None, "shots"),
        P(None, "shots"),
        P(None, "shots"),
        P("shots", None),
        P(),
    )
    return jax.shard_map(
        body,
        mesh=mesh,
        in_specs=placed,
        out_specs=(P(("shots", "gx"), "gy", None), P(("shots", "gx"), None, "gy")),
        check_vma=False,
    )
```
